32 devices in a mesh: sample: 4 (over y, core), tok: 8 (over z, x).
Axes of the slice: x: 2, y: 2, z: 4, core: 2. Of those that a mesh axis runs over, the one named last changes fastest.
Arguments:
- noisy_pos: float32 [4, 3, 4096], P('sample', None, 'tok'), may hold values from -384 to 384
- noise_step: int32 [1], replicated, may hold values from 60 to 120
- atom_single: bfloat16 [4096, 128], P('tok'), may hold values from -6 to 6
- atom_token: int32 [4096], P('tok'), may hold values from 0 to 511, as said below
- token_counts: int32 [512], P('tok'), may hold values from 1 to 29, as said below
- atom_bias: bfloat16 [4096, 2, 4, 128], P('tok'), may hold values from -400 to 400
- token_single: bfloat16 [512, 768], P('tok'), may hold values from -6 to 6
- pair_bias: bfloat16 [2, 16, 512, 512], P(None, 'sample', 'tok'), may hold values from -400 to 400
- w_pos: float32 [3, 128], replicated, may hold values from -3.5 to 3.5
- w_atom: bfloat16 [2, 128, 512], replicated, may hold values from -0.5 to 0.5
- w_atom_out: bfloat16 [2, 128, 128], replicated, may hold values from -0.5 to 0.5
- w_tok_in: bfloat16 [128, 768], replicated, may hold values from -0.5 to 0.5
- w_proj: bfloat16 [2, 3, 768, 768], replicated, may hold values from -0.21875 to 0.21875
- w_out: bfloat16 [2, 16, 48, 768], replicated, may hold values from -0.21875 to 0.21875
- w_tok_out: bfloat16 [768, 128], replicated, may hold values from -0.21875 to 0.21875
- w_pos_out: bfloat16 [3, 128], replicated, may hold values from -0.5 to 0.5
Outputs:
- denoised: float32 [4, 3, 4096], P('sample', None, 'tok')
The draws below stay inside these ranges and needn't reach their ends.
Inputs may be any that keep to these rules, and one draw needn't show every extreme that they name: Atoms are ordered by token: atom_token never falls, token t owns exactly token_counts[t] consecutive atoms, and every token owns one atom or more. `token_counts`: they sum to 4096; each of the first 128 tokens has 23 to 29 atoms, each other token 1 to 3; token 0 has 29.
All inputs are finite; a program needn't handle non-finite values.
Results may differ from the reference program's by a relative error of at most 0.012.
Values may be sent and summed in bfloat16 or wider, within the bound.
A program may use at most 128 MiB of HBM per device.

```python
import math
import jax
import jax.numpy as jnp
from jax import lax

CA = 128
AH = 4
CT = 768
TH = 16
WQ = 32
WK = 128
NB = 2
AL = 2
HD = 48
RIM = 80
TOKENS = 512
ATOMS = 4096
SAMPLES = 4


def token_layout(key):
    heavy = jnp.arange(TOKENS) < TOKENS // 4
    big_extra = jax.random.randint(jax.random.fold_in(key, 1), (TOKENS,), 0, 4)
    small_extra = jax.random.randint(jax.random.fold_in(key, 2), (TOKENS,), 0, 2)
    extra = jnp.where(heavy, big_extra, small_extra).astype(jnp.int32)
    extra = extra.at[0].set(3).at[TOKENS // 4 - 1].set(0).at[TOKENS - 1].set(0)
    before = jnp.concatenate([jnp.zeros((1,), jnp.int32), extra[:-1]])
    base = jnp.where(heavy, 26, 2).astype(jnp.int32)
    return (base + extra - before).astype(jnp.int32)


def draw_token_counts(key, part):
    return token_layout(key)


def draw_atom_token(key, part):
    counts = token_layout(key)
    ends = jnp.cumsum(counts)
    return jnp.searchsorted(ends, jnp.arange(ATOMS), side='right').astype(jnp.int32)


def draw_atom_bias(key, part):
    key = jax.random.fold_in(key, 11)
    shape = (ATOMS, AL, AH, WK)
    return jnp.clip(jax.random.normal(key, shape, jnp.float32), -6.0, 6.0).astype(jnp.bfloat16)


def draw_pair_bias(key, part):
    key = jax.random.fold_in(key, 23)
    shape = (NB, TH, TOKENS, TOKENS)
    return jnp.clip(jax.random.normal(key, shape, jnp.float32), -6.0, 6.0).astype(jnp.bfloat16)


def shard_levels(rng, dims, cuts, smallest, high):
    gain, own = 1.0, jax.random.fold_in(rng, 6)
    for dim, blocks in cuts:
        steps = jnp.exp(jax.random.uniform(jax.random.fold_in(own, dim), (blocks,), jnp.float32, smallest / len(cuts), high / len(cuts)))
        gain = gain * jnp.repeat(steps, dims[dim] // blocks).reshape([-1 if axis == dim else 1 for axis in range(len(dims))])
    return gain


def scatter_about(stream_key, dims, deviation, limit, cuts=(), kind=jnp.bfloat16):
    values = deviation * jax.random.normal(stream_key, dims, jnp.float32)
    if cuts:
        values = values * shard_levels(stream_key, dims, cuts, -0.22, 0.18)
    return jnp.clip(values, -limit, limit).astype(kind)


def setup_inputs(seed: int = 0) -> dict:
    seeds = jax.random.split(jax.random.key(seed), 17)
    noisy_pos = scatter_about(seeds[0], (SAMPLES, 3, ATOMS), 64.0, 384.0, ((0, 4), (2, 8)), jnp.float32)
    noise_step = jax.random.randint(seeds[1], (1,), 60, 121).astype(jnp.int32)
    atom_single = scatter_about(seeds[2], (ATOMS, CA), 1.0, 6.0, ((0, 8),))
    atom_token = draw_atom_token(jax.random.fold_in(seeds[16], 71), 0)
    token_counts = draw_token_counts(jax.random.fold_in(seeds[16], 71), 0)
    atom_bias = draw_atom_bias(jax.random.fold_in(seeds[16], 71), 0)
    token_single = scatter_about(seeds[6], (TOKENS, CT), 1.0, 6.0, ((0, 8),))
    pair_bias = draw_pair_bias(jax.random.fold_in(seeds[16], 71), 0)
    w_pos = scatter_about(seeds[8], (3, CA), 3 ** -0.5, 3.5, (), jnp.float32)
    w_atom = scatter_about(seeds[9], (AL, CA, 4 * CA), CA ** -0.5, 0.5)
    w_atom_out = scatter_about(seeds[10], (AL, CA, CA), CA ** -0.5, 0.5)
    w_tok_in = scatter_about(seeds[11], (CA, CT), CA ** -0.5, 0.5)
    w_proj = scatter_about(seeds[12], (NB, 3, CT, CT), CT ** -0.5, 0.21875)
    w_out = scatter_about(seeds[13], (NB, TH, HD, CT), CT ** -0.5, 0.21875)
    w_tok_out = scatter_about(seeds[14], (CT, CA), CT ** -0.5, 0.21875)
    w_pos_out = scatter_about(seeds[15], (3, CA), CA ** -0.5, 0.5)
    return dict(noisy_pos=noisy_pos, noise_step=noise_step, atom_single=atom_single, atom_token=atom_token, token_counts=token_counts, atom_bias=atom_bias, token_single=token_single, pair_bias=pair_bias, w_pos=w_pos, w_atom=w_atom, w_atom_out=w_atom_out, w_tok_in=w_tok_in, w_proj=w_proj, w_out=w_out, w_tok_out=w_tok_out, w_pos_out=w_pos_out)


sigma_data = 16.0
sigma_peak = 160.0
sigma_floor = 0.0004
plan_steps = 200.0
norm_eps = 1e-05
masked_score = -1000000000.0

def noise_level(noise_step):
    fraction = noise_step[0].astype(jnp.float32) / plan_steps
    upper = sigma_peak ** (1.0 / 7.0)
    lower = sigma_floor ** (1.0 / 7.0)
    return sigma_data * (upper + fraction * (lower - upper)) ** 7

def layer_norm(values):
    centred = values - lax.optimization_barrier(jnp.mean(values, axis=-1, keepdims=True))
    spread = lax.optimization_barrier(jnp.mean(centred * centred, axis=-1, keepdims=True))
    return centred / jnp.sqrt(spread + norm_eps)

def widen(values):
    return lax.optimization_barrier(values.astype(jnp.bfloat16)).astype(jnp.float32)

def key_windows(padded, windows):
    blocks = padded.reshape(-1, WQ, padded.shape[-1])
    pieces = [blocks[1 + offset:1 + offset + windows] for offset in range(WK // WQ)]
    return jnp.concatenate(pieces, axis=1)

def atom_layer(atom_act, weights, out_weights, bias):
    atom_count, width = atom_act.shape
    head_count = bias.shape[1]
    head_dim = width // head_count
    windows = atom_count // WQ
    normed = layer_norm(atom_act).astype(jnp.bfloat16)
    projected = jnp.dot(normed, weights, preferred_element_type=jnp.float32)
    query_rows = widen(projected[:, :width])
    key_rows = widen(projected[:, width:2 * width])
    value_rows = widen(projected[:, 2 * width:3 * width])
    gate_rows = projected[:, 3 * width:]
    padding = ((RIM, RIM), (0, 0))
    window_keys = key_windows(jnp.pad(key_rows, padding), windows).reshape(windows, WK, head_count, head_dim)
    window_values = key_windows(jnp.pad(value_rows, padding), windows).reshape(windows, WK, head_count, head_dim)
    window_queries = query_rows.reshape(windows, WQ, head_count, head_dim)
    score_scale = 1.0 / math.sqrt(head_dim)
    scores = jnp.einsum('wqhd,wkhd->whqk', window_queries, window_keys) * score_scale
    scores = scores + bias.reshape(windows, WQ, head_count, WK).transpose(0, 2, 1, 3).astype(jnp.float32)
    positions = WQ * jnp.arange(windows)[:, None] - (WK - WQ) // 2 + jnp.arange(WK)[None, :]
    valid = (positions >= 0) & (positions < atom_count)
    scores = jnp.where(valid[:, None, None, :], scores, masked_score)
    row_max = lax.optimization_barrier(jnp.max(scores, axis=-1, keepdims=True))
    exponent = jnp.exp(scores - row_max)
    mixed = jnp.einsum('whqk,wkhd->wqhd', widen(exponent), window_values)
    mixed = mixed / jnp.transpose(lax.optimization_barrier(jnp.sum(exponent, axis=-1, keepdims=True)), (0, 2, 1, 3))
    gated = (mixed.reshape(atom_count, width) * jax.nn.sigmoid(gate_rows)).astype(jnp.bfloat16)
    return atom_act + jnp.dot(gated, out_weights, preferred_element_type=jnp.float32)

def token_block(token_act, proj, out_weights, bias):
    head_count = bias.shape[0]
    head_dim = out_weights.shape[1]
    token_total = token_act.shape[0]
    normed = widen(layer_norm(token_act))
    projected = widen(jnp.einsum('tc,xcd->xtd', normed, proj.astype(jnp.float32)))
    grouped = projected.reshape(3, token_total, head_count, head_dim).transpose(2, 1, 0, 3).reshape(head_count, token_total, 3 * head_dim)
    score_scale = 1.0 / math.sqrt(head_dim)

    def one_head(item):
        block_rows, head_bias = item
        query_rows = block_rows[:, :head_dim]
        key_rows = block_rows[:, head_dim:2 * head_dim]
        value_rows = block_rows[:, 2 * head_dim:]
        scores = jnp.dot(query_rows, key_rows.T) * score_scale + head_bias.astype(jnp.float32)
        row_max = lax.optimization_barrier(jnp.max(scores, axis=1, keepdims=True))
        exponent = jnp.exp(scores - row_max)
        mixed = jnp.dot(widen(exponent), value_rows) / lax.optimization_barrier(jnp.sum(exponent, axis=1, keepdims=True))
        return widen(mixed)
    mixed = lax.map(one_head, (grouped, bias))
    return token_act + jnp.einsum('htd,hdc->tc', mixed, out_weights.astype(jnp.float32))

def reference(noisy_pos, noise_step, atom_single, atom_token, token_counts, atom_bias, token_single, pair_bias, w_pos, w_atom, w_atom_out, w_tok_in, w_proj, w_out, w_tok_out, w_pos_out):
    sigma = noise_level(noise_step)
    square = sigma * sigma + sigma_data * sigma_data
    scale_in = 1.0 / jnp.sqrt(square)
    scale_skip = sigma_data * sigma_data / square
    scale_out = sigma * sigma_data / jnp.sqrt(square)

    def one_sample(position):
        atom_act = atom_single.astype(jnp.float32) + jnp.dot((position * scale_in).T, w_pos, precision=lax.Precision.HIGHEST)
        for layer in range(w_atom.shape[0]):
            atom_act = atom_layer(atom_act, w_atom[layer], w_atom_out[layer], atom_bias[:, layer])
        lifted = widen(jax.nn.relu(atom_act))
        pooled = jax.ops.segment_sum(lifted, atom_token, num_segments=TOKENS)
        token_mean = (pooled / token_counts[:, None].astype(jnp.float32)).astype(jnp.bfloat16)
        token_act = token_single.astype(jnp.float32) + jnp.dot(token_mean, w_tok_in, preferred_element_type=jnp.float32)
        for block in range(w_proj.shape[0]):
            token_act = token_block(token_act, w_proj[block], w_out[block], pair_bias[block])
        token_emit = jnp.dot(layer_norm(token_act).astype(jnp.bfloat16), w_tok_out, preferred_element_type=jnp.float32).astype(jnp.bfloat16)
        atom_final = atom_act + token_emit[atom_token].astype(jnp.float32)
        atom_out = layer_norm(atom_final).astype(jnp.bfloat16)
        update = jnp.dot(w_pos_out, atom_out.T, preferred_element_type=jnp.float32)
        return (scale_skip * position + scale_out * update) / sigma_data
    return lax.map(one_sample, noisy_pos)
```

```python
import functools
import math

import jax
import jax.numpy as jnp
from jax import lax
from jax.experimental import pallas as pl
from jax.experimental.pallas import tpu as pltpu
from jax.sharding import PartitionSpec as P

WQ = 32
WK = 128
HALO = (WK - WQ) // 2

MESH = pl.DeviceIdType.MESH
sigma_data = 16.0
sigma_peak = 160.0
sigma_floor = 0.0004
plan_steps = 200.0
norm_eps = 1e-05
masked_score = -1000000000.0
BF = jnp.bfloat16
F32 = jnp.float32
ANY = pl.BlockSpec(memory_space=pl.ANY)
VMEM = pl.BlockSpec(memory_space=pltpu.VMEM)


def noise_level(noise_step):
    fraction = noise_step[0].astype(jnp.float32) / plan_steps
    upper = sigma_peak ** (1.0 / 7.0)
    lower = sigma_floor ** (1.0 / 7.0)
    return sigma_data * (upper + fraction * (lower - upper)) ** 7


def layer_norm(values):
    centred = values - jnp.mean(values, axis=-1, keepdims=True)
    spread = jnp.mean(centred * centred, axis=-1, keepdims=True)
    return centred * lax.rsqrt(spread + norm_eps)


def dot(a, b):
    return jnp.dot(a, b, preferred_element_type=F32)


def dot_t(a, b):
    return lax.dot_general(a, b, (((1,), (1,)), ((), ())), preferred_element_type=F32)


def head_mask(head, head_dim, width, kind):
    lane = lax.broadcasted_iota(jnp.int32, (1, width), 1)
    inside = (lane >= head * head_dim) & (lane < (head + 1) * head_dim)
    return jnp.where(inside, 1.0, 0.0).astype(kind)


def step_kernel(
    n,
    s_count,
    act0,
    tok_row,
    tok_col,
    counts,
    atom_bias,
    token_single,
    pair_bias,
    w_atom,
    w_atom_out,
    w_tok_in,
    w_proj_hbm,
    w_out_hbm,
    w_tok_out,
    w_pos_out,
    update_ref,
    act,
    kv,
    gated,
    part,
    pool_in,
    mean_all,
    single_all,
    bias_all,
    normed_all,
    emit_all,
    w_proj,
    w_out,
    weight_sem,
    halo_send,
    halo_recv,
    bias_send,
    bias_recv,
    single_send,
    single_recv,
    pool_send,
    pool_recv,
    mean_send,
    mean_recv,
    norm_send,
    norm_recv,
    emit_send,
    emit_recv,
):
    me = lax.axis_index("tok")
    mine = lax.axis_index("sample")
    layers, width = w_atom.shape[0], w_atom.shape[1]
    atoms = act0.shape[0]
    heads = atom_bias.shape[1] // (layers * WK)
    head_dim = width // heads
    local = token_single.shape[0]
    tokens = n * local
    sent = []

    def push(src, dst, send, recv, where):
        copy = pltpu.make_async_remote_copy(
            src_ref=src, dst_ref=dst, send_sem=send, recv_sem=recv,
            device_id=where, device_id_type=MESH,
        )
        copy.start()
        sent.append(copy)
        return copy

    def peer(distance):
        return lax.rem(me + distance, n)

    def rows_of(index):
        return pl.ds(pl.multiple_of(index * local, local), local)

    def spread_rows(src, dst, send, recv):
        return [
            push(src, dst.at[rows_of(me)], send.at[d - 1], recv.at[d - 1], {"tok": peer(d)})
            for d in range(1, n)
        ]

    weights = [
        pltpu.make_async_copy(w_proj_hbm, w_proj, weight_sem.at[0]),
        pltpu.make_async_copy(w_out_hbm, w_out, weight_sem.at[1]),
    ]
    for copy in weights:
        copy.start()

    barrier = pltpu.get_barrier_semaphore()
    for d in range(1, n):
        pl.semaphore_signal(barrier, inc=1, device_id={"tok": peer(d)}, device_id_type=MESH)
    for d in range(1, s_count):
        pl.semaphore_signal(
            barrier, inc=1, device_id={"sample": lax.rem(mine + d, s_count)}, device_id_type=MESH
        )
    pl.semaphore_wait(barrier, n - 1 + s_count - 1)

    bias_copies = [
        push(
            pair_bias, bias_all.at[mine], bias_send.at[d - 1], bias_recv.at[d - 1],
            {"sample": lax.rem(mine + d, s_count)},
        )
        for d in range(1, s_count)
    ]
    bias_all[mine] = pair_bias[...]

    act[...] = act0[...]
    windows = atoms // WQ
    first = me * atoms
    atom_total = n * atoms
    lane = lax.broadcasted_iota(jnp.int32, (1, WK), 1)
    atom_masks = [head_mask(h, head_dim, width, BF) for h in range(heads)]
    atom_masks32 = [head_mask(h, head_dim, width, F32) for h in range(heads)]
    score_scale = 1.0 / math.sqrt(head_dim)
    single_copies = []
    for layer in range(layers):
        normed = layer_norm(act[...]).astype(BF)
        proj = dot(normed, w_atom[layer])
        kv[layer, HALO : HALO + atoms, :] = proj[:, width : 3 * width].astype(BF)
        here = kv.at[layer]
        halo = [
            push(
                here.at[pl.ds(HALO, HALO)], here.at[pl.ds(HALO + atoms, HALO)],
                halo_send.at[layer, 0], halo_recv.at[layer, 0], {"tok": peer(n - 1)},
            ),
            push(
                here.at[pl.ds(atoms, HALO)], here.at[pl.ds(0, HALO)],
                halo_send.at[layer, 1], halo_recv.at[layer, 1], {"tok": peer(1)},
            ),
        ]
        if layer == 0:
            single_copies = spread_rows(token_single, single_all, single_send, single_recv)
            single_all[rows_of(me), :] = token_single[...]
        queries = proj[:, :width].astype(BF)
        gates = jax.nn.sigmoid(proj[:, 3 * width :])
        inner = [w for w in range(windows) if WQ * w >= HALO and WQ * w + WK <= HALO + atoms]
        outer = [w for w in range(windows) if w not in inner]
        for w in inner + outer:
            if outer and w == outer[0]:
                for copy in halo:
                    copy.wait_recv()
            low = WQ * w
            keys = kv[layer, low : low + WK, :width]
            values = kv[layer, low : low + WK, width:]
            q = queries[low : low + WQ]
            stacked = jnp.concatenate([q * m for m in atom_masks], axis=0)
            bias = jnp.concatenate(
                [
                    atom_bias[low : low + WQ, (layer * heads + h) * WK : (layer * heads + h + 1) * WK]
                    for h in range(heads)
                ],
                axis=0,
            )
            scores = dot_t(stacked, keys) * score_scale + bias.astype(F32)
            if w in outer:
                position = first + (WQ * w - HALO) + lane
                valid = (position >= 0) & (position < atom_total)
                scores = jnp.where(valid, scores, masked_score)
            exponent = jnp.exp(scores - jnp.max(scores, axis=-1, keepdims=True))
            inverse = 1.0 / jnp.sum(exponent, axis=-1, keepdims=True)
            mixed = dot(exponent.astype(BF), values) * inverse
            total = mixed[:WQ] * atom_masks32[0]
            for h in range(1, heads):
                total = total + mixed[h * WQ : (h + 1) * WQ] * atom_masks32[h]
            gated[low : low + WQ, :] = (total * gates[low : low + WQ]).astype(BF)
        act[...] = act[...] + dot(gated[...], w_atom_out[layer])

    lifted = jnp.maximum(act[...], 0.0).astype(BF)
    owner = lax.broadcasted_iota(jnp.int32, (tokens, atoms), 0)
    onehot = jnp.where(owner == tok_row[...], 1.0, 0.0).astype(BF)
    part[...] = dot(onehot, lifted).astype(BF)
    pool_copies = [
        push(
            part.at[rows_of(peer(d))], pool_in.at[d - 1], pool_send.at[d - 1],
            pool_recv.at[d - 1], {"tok": peer(d)},
        )
        for d in range(1, n)
    ]
    pooled = part[rows_of(me), :].astype(F32)
    for d in range(1, n):
        pool_copies[d - 1].wait_recv()
        pooled = pooled + pool_in[d - 1].astype(F32)
    mean_all[rows_of(me), :] = (pooled / counts[...]).astype(BF)
    mean_copies = spread_rows(mean_all.at[rows_of(me)], mean_all, mean_send, mean_recv)

    model = token_single.shape[1]
    token_head_dim = w_out.shape[1] // (s_count * pair_bias.shape[1])
    span = 3 * 128
    per_group = span // token_head_dim
    per_source = pair_bias.shape[1]
    token_scale = 1.0 / math.sqrt(token_head_dim)
    token_masks = [head_mask(h, token_head_dim, span, BF) for h in range(per_group)]
    token_masks32 = [head_mask(h, token_head_dim, span, F32) for h in range(per_group)]

    def token_block(block, everyone, ours):
        q = dot(ours, w_proj[block, 0]).astype(BF)
        k = dot(everyone, w_proj[block, 1]).astype(BF)
        v = dot(everyone, w_proj[block, 2]).astype(BF)
        delta = None
        for group in range(model // span):
            cut = slice(group * span, (group + 1) * span)
            qg, kg, vg = q[:, cut], k[:, cut], v[:, cut]
            total = None
            for source in range(group * per_group // per_source, (group + 1) * per_group // per_source):
                start = source * per_source - group * per_group
                stacked = jnp.concatenate(
                    [qg * token_masks[start + h] for h in range(per_source)], axis=0
                )
                bias = jnp.concatenate(
                    [bias_all[source, block, h] for h in range(per_source)], axis=0
                )
                scores = dot_t(stacked, kg) * token_scale + bias.astype(F32)
                exponent = jnp.exp(scores - jnp.max(scores, axis=-1, keepdims=True))
                inverse = 1.0 / jnp.sum(exponent, axis=-1, keepdims=True)
                mixed = dot(exponent.astype(BF), vg) * inverse
                for h in range(per_source):
                    term = mixed[h * local : (h + 1) * local] * token_masks32[start + h]
                    total = term if total is None else total + term
            term = dot(total.astype(BF), w_out[block, cut, :])
            delta = term if delta is None else delta + term
        return delta

    for copy in single_copies:
        copy.wait_recv()
    for copy in weights:
        copy.wait()
    for copy in mean_copies:
        copy.wait_recv()
    token_all = single_all[...].astype(F32) + dot(mean_all[...], w_tok_in[...])
    normed_all[0] = layer_norm(token_all).astype(BF)
    token_act = token_single[...].astype(F32) + dot(mean_all[rows_of(me), :], w_tok_in[...])
    for copy in bias_copies:
        copy.wait_recv()
    blocks = w_proj.shape[0]
    for block in range(blocks):
        ours = normed_all[block, rows_of(me), :]
        token_act = token_act + token_block(block, normed_all[block], ours)
        if block + 1 < blocks:
            normed_all[block + 1, rows_of(me), :] = layer_norm(token_act).astype(BF)
            landing = normed_all.at[block + 1]
            for copy in spread_rows(
                landing.at[rows_of(me)], landing, norm_send.at[block], norm_recv.at[block]
            ):
                copy.wait_recv()

    emit_all[rows_of(me), :] = dot(layer_norm(token_act).astype(BF), w_tok_out[...]).astype(BF)
    emit_copies = spread_rows(emit_all.at[rows_of(me)], emit_all, emit_send, emit_recv)
    owner = lax.broadcasted_iota(jnp.int32, (atoms, tokens), 1)
    onehot = jnp.where(owner == tok_col[...], 1.0, 0.0).astype(BF)
    for copy in emit_copies:
        copy.wait_recv()
    final = act[...] + dot(onehot, emit_all[...])
    update_ref[...] = dot_t(w_pos_out[...], layer_norm(final).astype(BF))
    for copy in sent:
        copy.wait_send()


def on_device(
    n,
    s_count,
    noisy_pos,
    noise_step,
    atom_single,
    atom_token,
    token_counts,
    atom_bias,
    token_single,
    pair_bias,
    w_pos,
    w_atom,
    w_atom_out,
    w_tok_in,
    w_proj,
    w_out,
    w_tok_out,
    w_pos_out,
):
    position = noisy_pos[0]
    atoms = position.shape[1]
    local, model = token_single.shape
    width = atom_single.shape[1]
    tokens = local * n
    layers = w_atom.shape[0]
    blocks = w_proj.shape[0]
    sigma = noise_level(noise_step)
    square = sigma * sigma + sigma_data * sigma_data
    scale_in = 1.0 / jnp.sqrt(square)
    scale_skip = sigma_data * sigma_data / square
    scale_out = sigma * sigma_data / jnp.sqrt(square)
    act0 = atom_single.astype(F32) + jnp.dot(
        jnp.transpose(position * scale_in), w_pos, precision=lax.Precision.HIGHEST
    )
    dma = pltpu.SemaphoreType.DMA
    update = pl.pallas_call(
        functools.partial(step_kernel, n, s_count),
        out_shape=jax.ShapeDtypeStruct((16, atoms), F32),
        in_specs=[VMEM] * 10 + [ANY] * 2 + [VMEM] * 2,
        out_specs=VMEM,
        scratch_shapes=[
            pltpu.VMEM((atoms, width), F32),
            pltpu.VMEM((layers, atoms + 2 * HALO, 2 * width), BF),
            pltpu.VMEM((atoms, width), BF),
            pltpu.VMEM((tokens, width), BF),
            pltpu.VMEM((n - 1, local, width), BF),
            pltpu.VMEM((tokens, width), BF),
            pltpu.VMEM((tokens, model), BF),
            pltpu.VMEM((s_count,) + pair_bias.shape, BF),
            pltpu.VMEM((blocks, tokens, model), BF),
            pltpu.VMEM((tokens, width), BF),
            pltpu.VMEM(w_proj.shape, BF),
            pltpu.VMEM((blocks, model, model), BF),
            dma((2,)),
            dma((layers, 2)),
            dma((layers, 2)),
            dma((s_count - 1,)),
            dma((s_count - 1,)),
            dma((n - 1,)),
            dma((n - 1,)),
            dma((n - 1,)),
            dma((n - 1,)),
            dma((n - 1,)),
            dma((n - 1,)),
            dma((blocks - 1, n - 1)),
            dma((blocks - 1, n - 1)),
            dma((n - 1,)),
            dma((n - 1,)),
        ],
        compiler_params=pltpu.CompilerParams(
            collective_id=0, has_side_effects=True, vmem_limit_bytes=58 * 2**20
        ),
    )(
        act0,
        atom_token.reshape(1, atoms),
        atom_token.reshape(atoms, 1),
        token_counts.astype(F32).reshape(local, 1),
        atom_bias.reshape(atoms, -1),
        token_single,
        pair_bias,
        w_atom,
        w_atom_out,
        w_tok_in,
        w_proj,
        w_out.reshape(blocks, model, model),
        w_tok_out,
        jnp.pad(w_pos_out, ((0, 16 - w_pos_out.shape[0]), (0, 0))),
    )[: position.shape[0]]
    return ((scale_skip * position + scale_out * update) / sigma_data)[None]


def solution(mesh):
    in_specs = (
        P("sample", None, "tok"),
        P(),
        P("tok", None),
        P("tok"),
        P("tok"),
        P("tok", None, None, None),
        P("tok", None),
        P(None, "sample", "tok", None),
        P(),
        P(),
        P(),
        P(),
        P(),
        P(),
        P(),
        P(),
    )
    return jax.shard_map(
        functools.partial(on_device, mesh.shape["tok"], mesh.shape["sample"]),
        mesh=mesh,
        in_specs=in_specs,
        out_specs=P("sample", None, "tok"),
        check_vma=False,
    )
```

```python
import functools
import math

import jax
import jax.numpy as jnp
from jax import lax
from jax.experimental import pallas as pl
from jax.experimental.pallas import tpu as pltpu
from jax.sharding import PartitionSpec as P

WQ = 32
WK = 128
HALO = (WK - WQ) // 2

MESH = pl.DeviceIdType.MESH
sigma_data = 16.0
sigma_peak = 160.0
sigma_floor = 0.0004
plan_steps = 200.0
norm_eps = 1e-05
masked_score = -1000000000.0
BF = jnp.bfloat16
F32 = jnp.float32
ANY = pl.BlockSpec(memory_space=pl.ANY)
VMEM = pl.BlockSpec(memory_space=pltpu.VMEM)


def noise_level(noise_step):
    fraction = noise_step.astype(jnp.float32) / plan_steps
    upper = sigma_peak ** (1.0 / 7.0)
    lower = sigma_floor ** (1.0 / 7.0)
    return sigma_data * (upper + fraction * (lower - upper)) ** 7


def layer_norm(values):
    centred = values - jnp.mean(values, axis=-1, keepdims=True)
    spread = jnp.mean(centred * centred, axis=-1, keepdims=True)
    return centred * lax.rsqrt(spread + norm_eps)


def dot(a, b):
    return jnp.dot(a, b, preferred_element_type=F32)


def dot_t(a, b):
    return lax.dot_general(a, b, (((1,), (1,)), ((), ())), preferred_element_type=F32)


def head_mask(head, head_dim, width, kind):
    lane = lax.broadcasted_iota(jnp.int32, (1, width), 1)
    inside = (lane >= head * head_dim) & (lane < (head + 1) * head_dim)
    return jnp.where(inside, 1.0, 0.0).astype(kind)


def step_kernel(
    n,
    s_count,
    noise_step,
    noisy_pos,
    atom_single,
    tok_row,
    counts,
    atom_bias,
    token_single,
    pair_bias,
    w_pos,
    w_atom,
    w_atom_out,
    w_tok_in,
    w_proj_hbm,
    w_out_hbm,
    w_tok_out,
    w_pos_out,
    out_ref,
    act,
    kv,
    gated,
    part,
    pool_in,
    mean_all,
    single_all,
    bias_all,
    normed_all,
    emit_all,
    w_proj,
    w_out,
    weight_sem,
    halo_send,
    halo_recv,
    bias_send,
    bias_recv,
    single_send,
    single_recv,
    relay_send,
    relay_recv,
    pool_send,
    pool_recv,
    mean_send,
    mean_recv,
    norm_send,
    norm_recv,
    emit_send,
    emit_recv,
):
    me = lax.axis_index("tok")
    mine = lax.axis_index("sample")
    layers, width = w_atom.shape[0], w_atom.shape[1]
    atoms = atom_single.shape[0]
    heads = atom_bias.shape[0] // (atoms * layers)
    head_dim = width // heads
    local = token_single.shape[0]
    tokens = n * local
    sent = []

    def push(src, dst, send, recv, where):
        copy = pltpu.make_async_remote_copy(
            src_ref=src, dst_ref=dst, send_sem=send, recv_sem=recv,
            device_id=where, device_id_type=MESH,
        )
        copy.start()
        sent.append(copy)
        return copy

    def peer(distance):
        return lax.rem(me + distance, n)

    def rows_of(index):
        return pl.ds(pl.multiple_of(index * local, local), local)

    def spread_rows(src, dst, send, recv):
        return [
            push(src, dst.at[rows_of(me)], send.at[d - 1], recv.at[d - 1], {"tok": peer(d)})
            for d in range(1, n)
        ]

    def relay_rows(landing, send, recv):
        partner = me + 1 - 2 * lax.rem(me, 2)
        half = n // 2

        def hand(index, slot, target):
            block = landing.at[rows_of(index)]
            return push(block, block, send.at[slot], recv.at[slot], {"tok": target})

        beside = [hand(me, 0, partner)]
        along = [hand(me, i, peer(2 * i)) for i in range(1, half)]
        for i in range(1, half):
            along[i - 1].wait_recv()
            beside.append(hand(peer(n - 2 * i), half - 1 + i, partner))
        for copy in beside:
            copy.wait_recv()

    weights = [
        pltpu.make_async_copy(w_proj_hbm, w_proj, weight_sem.at[0]),
        pltpu.make_async_copy(w_out_hbm, w_out, weight_sem.at[1]),
    ]
    for copy in weights:
        copy.start()

    barrier = pltpu.get_barrier_semaphore()
    for d in range(1, n):
        pl.semaphore_signal(barrier, inc=1, device_id={"tok": peer(d)}, device_id_type=MESH)
    for d in range(1, s_count):
        pl.semaphore_signal(
            barrier, inc=1, device_id={"sample": lax.rem(mine + d, s_count)}, device_id_type=MESH
        )
    pl.semaphore_wait(barrier, n - 1 + s_count - 1)

    def send_bias(block):
        return [
            push(
                pair_bias.at[block], bias_all.at[mine, block], bias_send.at[block, d - 1],
                bias_recv.at[block, d - 1], {"sample": lax.rem(mine + d, s_count)},
            )
            for d in range(1, s_count)
        ]

    bias_copies = [send_bias(0)]
    bias_all[mine] = pair_bias[...]

    shares, share_rows = single_all.shape[1], single_all.shape[2]
    share = lax.rem(mine, shares)
    share_at = pl.ds(pl.multiple_of(share * share_rows, share_rows), share_rows)

    sigma = noise_level(jnp.full((1, 1), noise_step[0], jnp.int32))
    square = sigma * sigma + sigma_data * sigma_data
    position = noisy_pos[0]
    act[...] = atom_single[...].astype(F32) + lax.dot_general(
        position * (1.0 / jnp.sqrt(square)), w_pos[...], (((0,), (0,)), ((), ())),
        precision=lax.Precision.HIGHEST, preferred_element_type=F32,
    )
    stacked_row = lax.broadcasted_iota(jnp.int32, (heads * WQ, WQ * layers * heads), 0)
    bias_row = lax.broadcasted_iota(jnp.int32, (heads * WQ, WQ * layers * heads), 1)
    wanted = (stacked_row & (WQ - 1)) * (layers * heads) + lax.shift_right_logical(stacked_row, 5)
    windows = atoms // WQ
    first = me * atoms
    atom_total = n * atoms
    lane = lax.broadcasted_iota(jnp.int32, (1, WK), 1)
    atom_masks = [head_mask(h, head_dim, width, BF) for h in range(heads)]
    atom_masks32 = [head_mask(h, head_dim, width, F32) for h in range(heads)]
    score_scale = 1.0 / math.sqrt(head_dim)
    single_copies = []
    for layer in range(layers):
        normed = layer_norm(act[...]).astype(BF)
        proj = dot(normed, w_atom[layer])
        kv[layer, HALO : HALO + atoms, :] = proj[:, width : 3 * width].astype(BF)
        here = kv.at[layer]
        halo = [
            push(
                here.at[pl.ds(HALO, HALO)], here.at[pl.ds(HALO + atoms, HALO)],
                halo_send.at[layer, 0], halo_recv.at[layer, 0], {"tok": peer(n - 1)},
            ),
            push(
                here.at[pl.ds(atoms, HALO)], here.at[pl.ds(0, HALO)],
                halo_send.at[layer, 1], halo_recv.at[layer, 1], {"tok": peer(1)},
            ),
        ]
        if layer == 0:
            single_copies = [
                push(
                    token_single.at[share_at], single_all.at[me, share],
                    single_send.at[d - 1], single_recv.at[d - 1], {"tok": peer(d)},
                )
                for d in range(1, n)
            ]
            single_all[me, share] = token_single[share_at, :]
        chooser = jnp.where(bias_row == wanted + layer * heads, 1.0, 0.0).astype(BF)
        queries = proj[:, :width].astype(BF)
        gates = jax.nn.sigmoid(proj[:, 3 * width :])
        inner = [w for w in range(windows) if WQ * w >= HALO and WQ * w + WK <= HALO + atoms]
        outer = [w for w in range(windows) if w not in inner]
        for w in inner + outer:
            if outer and w == outer[0]:
                for copy in halo:
                    copy.wait_recv()
            low = WQ * w
            keys = kv[layer, low : low + WK, :width]
            values = kv[layer, low : low + WK, width:]
            q = queries[low : low + WQ]
            stacked = jnp.concatenate([q * m for m in atom_masks], axis=0)
            tall = WQ * layers * heads
            bias = dot(chooser, atom_bias[w * tall : (w + 1) * tall, :])
            scores = dot_t(stacked, keys) * score_scale + bias
            if w in outer:
                place = first + (WQ * w - HALO) + lane
                valid = (place >= 0) & (place < atom_total)
                scores = jnp.where(valid, scores, masked_score)
            exponent = jnp.exp(scores - jnp.max(scores, axis=-1, keepdims=True))
            inverse = 1.0 / jnp.sum(exponent, axis=-1, keepdims=True)
            mixed = dot(exponent.astype(BF), values) * inverse
            total = mixed[:WQ] * atom_masks32[0]
            for h in range(1, heads):
                total = total + mixed[h * WQ : (h + 1) * WQ] * atom_masks32[h]
            gated[low : low + WQ, :] = (total * gates[low : low + WQ]).astype(BF)
        act[...] = act[...] + dot(gated[...], w_atom_out[layer])
        if layer == 0:
            for copy in single_copies:
                copy.wait_recv()
            relay_copies = [
                push(
                    single_all.at[:, share], single_all.at[:, share],
                    relay_send.at[d - 1], relay_recv.at[d - 1],
                    {"sample": mine - share + lax.rem(share + d, shares)},
                )
                for d in range(1, shares)
            ]
            for block in range(1, pair_bias.shape[0]):
                bias_copies.append(send_bias(block))

    lifted = jnp.maximum(act[...], 0.0).astype(BF)
    owner = lax.broadcasted_iota(jnp.int32, (tokens, atoms), 0)
    onehot = jnp.where(owner == tok_row[...], 1.0, 0.0).astype(BF)
    part[...] = dot(onehot, lifted).astype(BF)
    pool_copies = [
        push(
            part.at[rows_of(peer(d))], pool_in.at[d - 1], pool_send.at[d - 1],
            pool_recv.at[d - 1], {"tok": peer(d)},
        )
        for d in range(1, n)
    ]
    pooled = part[rows_of(me), :].astype(F32)
    for d in range(1, n):
        pool_copies[d - 1].wait_recv()
        pooled = pooled + pool_in[d - 1].astype(F32)
    diagonal = lax.broadcasted_iota(jnp.int32, (local, local), 0) == lax.broadcasted_iota(
        jnp.int32, (local, local), 1
    )
    divisor = jnp.sum(
        jnp.where(diagonal, counts[...].astype(F32), 0.0), axis=1, keepdims=True
    )
    mean_all[rows_of(me), :] = (pooled / divisor).astype(BF)
    mean_copies = spread_rows(mean_all.at[rows_of(me)], mean_all, mean_send, mean_recv)

    model = token_single.shape[1]
    token_head_dim = w_out.shape[1] // (s_count * pair_bias.shape[1])
    span = 3 * 128
    per_group = span // token_head_dim
    per_source = pair_bias.shape[1]
    token_scale = 1.0 / math.sqrt(token_head_dim)
    token_masks = [head_mask(h, token_head_dim, span, BF) for h in range(per_group)]
    token_masks32 = [head_mask(h, token_head_dim, span, F32) for h in range(per_group)]

    def token_block(block, everyone, ours):
        q = dot(ours, w_proj[block, 0]).astype(BF)
        k = dot(everyone, w_proj[block, 1]).astype(BF)
        v = dot(everyone, w_proj[block, 2]).astype(BF)
        delta = None
        for group in range(model // span):
            cut = slice(group * span, (group + 1) * span)
            qg, kg, vg = q[:, cut], k[:, cut], v[:, cut]
            total = None
            for source in range(group * per_group // per_source, (group + 1) * per_group // per_source):
                start = source * per_source - group * per_group
                stacked = jnp.concatenate(
                    [qg * token_masks[start + h] for h in range(per_source)], axis=0
                )
                bias = jnp.concatenate(
                    [bias_all[source, block, h] for h in range(per_source)], axis=0
                )
                scores = dot_t(stacked, kg) * token_scale + bias.astype(F32)
                exponent = jnp.exp(scores - jnp.max(scores, axis=-1, keepdims=True))
                inverse = 1.0 / jnp.sum(exponent, axis=-1, keepdims=True)
                mixed = dot(exponent.astype(BF), vg) * inverse
                for h in range(per_source):
                    term = mixed[h * local : (h + 1) * local] * token_masks32[start + h]
                    total = term if total is None else total + term
            term = dot(total.astype(BF), w_out[block, cut, :])
            delta = term if delta is None else delta + term
        return delta

    for copy in relay_copies:
        copy.wait_recv()
    for copy in weights:
        copy.wait()
    for copy in mean_copies:
        copy.wait_recv()
    token_all = single_all[...].reshape(tokens, model).astype(F32) + dot(mean_all[...], w_tok_in[...])
    normed_all[0] = layer_norm(token_all).astype(BF)
    token_act = token_single[...].astype(F32) + dot(mean_all[rows_of(me), :], w_tok_in[...])
    blocks = w_proj.shape[0]
    for block in range(blocks):
        for copy in bias_copies[block]:
            copy.wait_recv()
        ours = normed_all[block, rows_of(me), :]
        token_act = token_act + token_block(block, normed_all[block], ours)
        if block + 1 < blocks:
            normed_all[block + 1, rows_of(me), :] = layer_norm(token_act).astype(BF)
            relay_rows(normed_all.at[block + 1], norm_send.at[block], norm_recv.at[block])

    emit_all[rows_of(me), :] = dot(layer_norm(token_act).astype(BF), w_tok_out[...]).astype(BF)
    emit_copies = spread_rows(emit_all.at[rows_of(me)], emit_all, emit_send, emit_recv)
    for copy in emit_copies:
        copy.wait_recv()
    final = act[...] + lax.dot_general(
        onehot, emit_all[...], (((0,), (0,)), ((), ())), preferred_element_type=F32
    )
    update = dot_t(w_pos_out[...], layer_norm(final).astype(BF))
    scale_skip = sigma_data * sigma_data / square
    scale_out = sigma * sigma_data / jnp.sqrt(square)
    out_ref[0] = (scale_skip * position + scale_out * update) / sigma_data
    for copy in sent:
        copy.wait_send()


def on_device(
    n,
    s_count,
    noisy_pos,
    noise_step,
    atom_single,
    atom_token,
    token_counts,
    atom_bias,
    token_single,
    pair_bias,
    w_pos,
    w_atom,
    w_atom_out,
    w_tok_in,
    w_proj,
    w_out,
    w_tok_out,
    w_pos_out,
):
    atoms = noisy_pos.shape[2]
    local, model = token_single.shape
    width = atom_single.shape[1]
    tokens = local * n
    layers = w_atom.shape[0]
    blocks = w_proj.shape[0]
    shares = 4 if s_count % 4 == 0 else s_count
    dma = pltpu.SemaphoreType.DMA
    return pl.pallas_call(
        functools.partial(step_kernel, n, s_count),
        out_shape=jax.ShapeDtypeStruct(noisy_pos.shape, F32),
        in_specs=[pl.BlockSpec(memory_space=pltpu.SMEM)] + [VMEM] * 11 + [ANY] * 2 + [VMEM] * 2,
        out_specs=VMEM,
        scratch_shapes=[
            pltpu.VMEM((atoms, width), F32),
            pltpu.VMEM((layers, atoms + 2 * HALO, 2 * width), BF),
            pltpu.VMEM((atoms, width), BF),
            pltpu.VMEM((tokens, width), BF),
            pltpu.VMEM((n - 1, local, width), BF),
            pltpu.VMEM((tokens, width), BF),
            pltpu.VMEM((n, shares, local // shares, model), BF),
            pltpu.VMEM((s_count,) + pair_bias.shape, BF),
            pltpu.VMEM((blocks, tokens, model), BF),
            pltpu.VMEM((tokens, width), BF),
            pltpu.VMEM(w_proj.shape, BF),
            pltpu.VMEM((blocks, model, model), BF),
            dma((2,)),
            dma((layers, 2)),
            dma((layers, 2)),
            dma((blocks, s_count - 1)),
            dma((blocks, s_count - 1)),
            dma((n - 1,)),
            dma((n - 1,)),
            dma((shares - 1,)),
            dma((shares - 1,)),
            dma((n - 1,)),
            dma((n - 1,)),
            dma((n - 1,)),
            dma((n - 1,)),
            dma((blocks - 1, n - 1)),
            dma((blocks - 1, n - 1)),
            dma((n - 1,)),
            dma((n - 1,)),
        ],
        compiler_params=pltpu.CompilerParams(
            collective_id=0, has_side_effects=True, vmem_limit_bytes=58 * 2**20
        ),
    )(
        noise_step,
        noisy_pos,
        atom_single,
        atom_token.reshape(1, atoms),
        token_counts.reshape(1, local),
        atom_bias.reshape(-1, WK),
        token_single,
        pair_bias,
        w_pos,
        w_atom,
        w_atom_out,
        w_tok_in,
        w_proj,
        w_out.reshape(blocks, model, model),
        w_tok_out,
        w_pos_out,
    )


def solution(mesh):
    in_specs = (
        P("sample", None, "tok"),
        P(),
        P("tok", None),
        P("tok"),
        P("tok"),
        P("tok", None, None, None),
        P("tok", None),
        P(None, "sample", "tok", None),
        P(),
        P(),
        P(),
        P(),
        P(),
        P(),
        P(),
        P(),
    )
    return jax.shard_map(
        functools.partial(on_device, mesh.shape["tok"], mesh.shape["sample"]),
        mesh=mesh,
        in_specs=in_specs,
        out_specs=P("sample", None, "tok"),
        check_vma=False,
    )
```
